32 devices in a mesh: lat: 4 (over z), lon: 8 (over y, x, core).
Axes of the slice: x: 2, y: 2, z: 4, core: 2. Of those that a mesh axis runs over, the one named last changes fastest.
Arguments:
- state: bfloat16 [256, 1440, 320], P('lat', 'lon'), may hold values from -6 to 6
- cutoff: int32 [128], replicated, may hold values from 90 to 719
- viscosity: float32 [320], replicated, may hold values from 0.02 to 0.2
Outputs:
- updated: float32 [256, 1440, 320], P('lat', 'lon')
The draws below stay inside these ranges and needn't reach their ends.
All inputs are finite; a program needn't handle non-finite values.
Results may differ from the reference program's by a relative error of at most 0.0033.
Values may be sent and summed in bfloat16 or wider, within the bound.
No kernel may reach another device: no remote copies, remote signals or barrier semaphores. Data moves between devices by JAX's collectives and lax.ppermute only.
A program may use at most 128 MiB of HBM per device.

```python
import math
import jax
import jax.numpy as jnp
from jax import lax

NLON = 1440
C = 320
NLAT = 256
NPOLAR = 128


def touch_ends(values, key, low, top_value):
    shape = values.shape
    spot = [jax.random.randint(jax.random.fold_in(key, axis), (), 0, shape[axis]) for axis in range(len(shape))]
    values = values.at[tuple(spot)].set(low)
    longest = shape.index(max(shape))
    spot[longest] = (spot[longest] + 1) % shape[longest]
    return values.at[tuple(spot)].set(top_value)


def steps_of(rng, dims, split, smallest, largest):
    def one(axis_at, shards_of):
        steps = jax.random.uniform(jax.random.fold_in(jax.random.fold_in(rng, 6), axis_at), (shards_of,), jnp.float32, smallest / len(split), largest / len(split))
        return jnp.repeat(jnp.exp(steps), dims[axis_at] // shards_of).reshape((-1,) + (1,) * (len(dims) - axis_at - 1))

    level = one(*split[0])
    for cut in split[1:]:
        level = level * one(*cut)
    return level


def centred(rng, shape, deviation, bound, cuts=(), kind=jnp.bfloat16):
    loudness = steps_of(rng, shape, cuts, -0.22, 0.18) if cuts else 1.0
    drawn = jax.random.normal(rng, shape, jnp.float32) * deviation * loudness
    return jnp.minimum(jnp.maximum(drawn, -bound), bound).astype(kind)


def setup_inputs(seed: int = 0) -> dict:
    seeds = jax.random.split(jax.random.key(seed), 4)
    return {
        "state": centred(seeds[0], (NLAT, NLON, C), 1.0, 6.0, ((0, 4), (1, 8))),
        "cutoff": touch_ends(jax.random.randint(seeds[1], (NPOLAR,), NLON // 16, NLON // 2), jax.random.fold_in(seeds[1], 1), NLON // 16, (NLON // 2) - 1).astype(jnp.int32),
        "viscosity": jnp.clip(jnp.exp(jax.random.uniform(seeds[2], (C,), jnp.float32, math.log(0.02), math.log(0.2))), 0.02, 0.2),
    }


def fourier_table(length):
    column = jnp.arange(length, dtype=jnp.int32)
    half_len = length // 2
    wavenumber = jnp.where(column <= half_len, column, column - half_len).astype(jnp.int32)
    product = (column[:, None] * wavenumber[None, :]) % length
    angles = product.astype(jnp.float32) * jnp.float32(2.0 * math.pi / length)
    fourier = jnp.where((column <= half_len)[None, :], jnp.cos(angles), jnp.sin(angles))
    weights = jnp.where((column == 0) | (column == half_len), jnp.float32(1.0 / length), jnp.float32(2.0 / length))
    return fourier.astype(jnp.bfloat16), wavenumber, weights.astype(jnp.float32)


def filter_block(row_block, cut_rows, fourier, wavenumber, weights):
    basis = fourier.astype(jnp.float32)
    spectrum = jnp.einsum("jk,rjc->rkc", basis, row_block.astype(jnp.float32), precision=lax.Precision.HIGHEST)
    retain = (wavenumber[None, :] <= cut_rows[:, None]).astype(jnp.float32) * weights[None, :]
    damped = (spectrum * retain[:, :, None]).astype(jnp.bfloat16)
    result = jnp.einsum("jk,rkc->rjc", basis, damped.astype(jnp.float32), precision=lax.Precision.HIGHEST)
    return result.astype(jnp.bfloat16)


def metric(global_rows, nlat):
    spacing = jnp.float32(math.pi / nlat)
    rows_f = global_rows.astype(jnp.float32)
    cell_cos = jnp.sin((rows_f + 0.5) * spacing)
    north_cos = jnp.where(global_rows == 0, jnp.float32(0.0), jnp.sin(rows_f * spacing))
    south_cos = jnp.where(global_rows == nlat - 1, jnp.float32(0.0), jnp.sin((rows_f + 1.0) * spacing))
    return north_cos / cell_cos, south_cos / cell_cos


def reference(state, cutoff, viscosity):
    nlat = state.shape[0]
    quarter = nlat // 4
    fourier, wavenumber, weights = fourier_table(NLON)
    polar_rows = jnp.concatenate([state[:quarter], state[nlat - quarter:]], axis=0)

    def one_row(element_pair):
        return filter_block(element_pair[0][None], element_pair[1][None], fourier, wavenumber, weights)[0]

    finished = lax.map(one_row, (polar_rows, cutoff))
    filtered = jnp.concatenate([finished[:quarter], state[quarter:nlat - quarter], finished[quarter:]], axis=0)
    fields = filtered.astype(jnp.float32)
    east_q = jnp.roll(fields, -1, axis=1)
    west_q = jnp.roll(fields, 1, axis=1)
    zeros_row = jnp.zeros_like(fields[:1])
    north_q = jnp.concatenate([zeros_row, fields[:-1]], axis=0)
    south_q = jnp.concatenate([fields[1:], zeros_row], axis=0)
    north_ratio, south_ratio = metric(jnp.arange(nlat, dtype=jnp.int32), nlat)
    viscous = viscosity[None, None, :]
    updated = fields + viscous * (east_q - 2.0 * fields + west_q)
    updated = updated + viscous * (north_ratio[:, None, None] * (north_q - fields) - south_ratio[:, None, None] * (fields - south_q))
    return updated
```

```python
import functools
import math

import jax
import jax.numpy as jnp
import ml_dtypes
import numpy as np
from jax import lax
from jax.experimental import pallas as pl
from jax.experimental.pallas import tpu as pltpu
from jax.sharding import PartitionSpec as P

NLON = 1440
MAIN = 256
TAIL = 64
BF = jnp.bfloat16
F32 = jnp.float32
ANY = pl.BlockSpec(memory_space=pl.ANY)
IN_SMEM = pl.BlockSpec(memory_space=pltpu.SMEM)
IN_VMEM = pl.BlockSpec(memory_space=pltpu.VMEM)


def table_pair(count, cols, pad, parity):
    half = NLON // 2
    turns = np.arange(NLON, dtype=np.float32) * np.float32(2.0 * math.pi / NLON)
    cos, sin = np.cos(turns).astype(np.float32), np.sin(turns).astype(np.float32)
    even = np.arange(parity, half + 1, 2)
    odd = even[(even > 0) & (even < half)]
    modes = np.concatenate([even, odd])
    is_cos = np.arange(modes.size) < even.size

    def rows(extra):
        place, live = [], []
        for block in range(count // 2):
            base = block * cols - extra
            used = cols + 2 * extra
            place += [base + i for i in range(used)] + [0] * (pad - used)
            live += [1] * used + [0] * (pad - used)
        turn = (np.array(place)[:, None] % NLON) * modes[None, :] % NLON
        return np.where(is_cos[None, :], cos[turn], sin[turn]) * np.array(live, np.float32)[:, None]

    forward = np.ascontiguousarray(rows(0).T).astype(ml_dtypes.bfloat16)
    return forward, rows(1).astype(ml_dtypes.bfloat16)


def copies(pairs, sems, base=0):
    made = [pltpu.make_async_copy(a, b, sems.at[base + i]) for i, (a, b) in enumerate(pairs)]
    for c in made:
        c.start()
    return made


def wait_all(made):
    for c in made:
        c.wait()


def pack_kernel(cols, pad, count, sets, s, *refs):
    me = s[0]
    n = len(sets)
    x, outs, (raw, work, in_sem, out_sem) = refs[0], refs[1 : 1 + 2 * n], refs[1 + 2 * n :]
    kinds = [(u, i, kind, q) for u, units in enumerate(sets) for i, (kind, q) in enumerate(units)]
    spots, at = [], 0
    for _, _, kind, q in kinds:
        size = count if kind == "main" else 4 * count
        spots.append((q * size, at, size))
        at += size
    loads = copies([(x.at[:, pl.ds(src, size), :], raw.at[:, pl.ds(dst, size), :]) for src, dst, size in spots], in_sem)
    stores = []
    for k, (u, i, kind, _) in enumerate(kinds):
        loads[k].wait()
        dst = spots[k][1]
        if kind == "main":
            flat = raw[:, dst : dst + count, :MAIN]
        else:
            flat = jnp.concatenate(
                [raw[:, dst + t * count : dst + (t + 1) * count, MAIN : MAIN + TAIL] for t in range(4)], axis=-1
            )
        turned = jnp.swapaxes(flat, 0, 1)
        for d in range(count):
            work[k, d, :cols] = turned[d]
            work[k, d, cols:] = jnp.zeros((pad - cols, MAIN), BF)
        lanes = pl.ds(i * MAIN, MAIN)
        pairs = []
        for m in range(count // 2):
            pairs.append((work.at[k, jnp.bitwise_xor(me, 2 * m)], outs[2 * u].at[m, :, lanes]))
            pairs.append((work.at[k, jnp.bitwise_xor(me, 2 * m + 1)], outs[2 * u + 1].at[m, :, lanes]))
        stores += copies(pairs, out_sem, k * count)
    wait_all(stores)


def select_kernel(groups, s, *refs):
    ins, ys, (held, in_sem, out_sem) = refs[: -groups - 3], refs[-groups - 3 : -3], refs[-3:]

    def move(own, par):
        spots = [(m, k) for m in range(groups) for k in range(2)]
        loads = copies([((own, par)[k].at[m], held.at[m, k]) for m, k in spots], in_sem)
        stores = []
        for m in range(groups):
            loads[2 * m].wait()
            loads[2 * m + 1].wait()
            stores += copies([(held.at[m], ys[m])], out_sem, m)
        wait_all(stores)

    if len(ins) == 2:
        move(*ins)
        return

    @pl.when(s[1] == 1)
    def _():
        move(*ins[:2])

    @pl.when(s[1] != 1)
    def _():
        move(*ins[2:])


def filter_kernel(groups, s, cut, *refs):
    me = s[0]
    ins, tables, zs = refs[:groups], refs[groups : groups + 4], refs[groups + 4 : 2 * groups + 4]
    work, done, held, in_sem, table_sem, out_sem = refs[2 * groups + 4 :][0:2] + (refs[2 * groups + 6 : -3],) + refs[-3:]
    count, pad, lanes = work.shape
    half = count // 2
    pairs = []
    for m in range(groups):
        for k in range(2):
            pairs.append((ins[m].at[k], work.at[jnp.bitwise_xor(me, 2 * m + k)]))
    loads = copies(pairs, in_sem)
    table_loads = copies(list(zip(tables, held)), table_sem)
    wait_all(loads)
    low = work[:half].astype(F32)
    high = work[half:].astype(F32)
    cutoff = cut[...]

    def side(values, parity):
        values = values.reshape(half * pad, lanes).astype(BF)
        table_loads[2 * parity].wait()
        forward = held[2 * parity]
        spectrum = jnp.dot(forward[...], values, preferred_element_type=F32)
        index = lax.broadcasted_iota(jnp.int32, (forward.shape[0], 1), 0)
        cosines = NLON // 4 + 1 - parity
        mode = jnp.where(index < cosines, 2 * index + parity, 2 * (index - cosines) + 2 - parity)
        weight = jnp.where((mode == 0) | (mode == NLON // 2), F32(1.0 / NLON), F32(2.0 / NLON))
        damped = (spectrum * jnp.where(mode <= cutoff, weight, F32(0.0))).astype(BF)
        table_loads[2 * parity + 1].wait()
        return jnp.dot(held[2 * parity + 1][...], damped, preferred_element_type=F32)

    even = side(low + high, 0)
    odd = side(low - high, 1)
    done[:half] = (even + odd).reshape(half, pad, lanes).astype(BF)
    done[half:] = (even - odd).reshape(half, pad, lanes).astype(BF)
    pairs = []
    for m in range(groups):
        for k in range(2):
            pairs.append((done.at[jnp.bitwise_xor(me, 2 * m + k)], zs[m].at[k]))
    wait_all(copies(pairs, out_sem))


def gather_kernel(groups, s, *refs):
    ins, outs, (held, in_sem, out_sem) = refs[:groups], refs[groups : groups + 2], refs[groups + 2 :]
    loads = copies([(ins[m], held.at[m]) for m in range(groups)], in_sem)
    stores = []
    for m in range(groups):
        loads[m].wait()
        stores += copies([(held.at[m, k], outs[k].at[m]) for k in range(2)], out_sem, 2 * m)
    wait_all(stores)


def row_of(own, par, rel):
    spot = lax.shift_right_logical(rel, 1)
    return jnp.where(jnp.bitwise_and(rel, 1) == 0, own[spot], par[spot])


def edge_kernel(cols, s, fo, fp, lo, lp, fto, ftp, lto, ltp, x_first, x_last, out_first, out_last):
    me, polar = s[0], s[1]
    count = x_first.shape[1]

    @pl.when(polar == 1)
    def _():
        for spot, own, par, tail_own, tail_par, at, out in (
            (0, fo, fp, fto, ftp, 0, out_first),
            (count - 1, lo, lp, lto, ltp, MAIN - TAIL, out_last),
        ):
            rel = jnp.bitwise_xor(me, spot)
            out[...] = jnp.concatenate(
                [row_of(own, par, rel), row_of(tail_own, tail_par, rel)[:, at : at + TAIL]], axis=-1
            )[1 : cols + 1]

    @pl.when(polar != 1)
    def _():
        out_first[...] = x_first[:, 0, :]
        out_last[...] = x_last[:, count - 1, :]


def final_kernel(cols, count, tiles, places, s, north, south, sides, coef, *refs):
    tails = tiles // 4
    parts, (x, out) = refs[:-11], refs[-11:-9]
    block, tail, own_rows, field, result, block_sem, tail_sem, row_sem, out_sem = refs[-9:]
    me, polar = s[0], s[1]
    width = 15
    groups = count // 2

    def sources(unit, place):
        number, i = places[unit]
        lanes = pl.ds(i * MAIN, MAIN)
        pairs = []
        for m in range(groups):
            for k in range(2):
                pairs.append((parts[2 * number + k].at[m, :, lanes], place(jnp.bitwise_xor(me, 2 * m + k))))
        return pairs

    def main_copies(q):
        slot = q % 2
        pairs = sources(("main", q), lambda d: block.at[slot, d])
        return [pltpu.make_async_copy(a, b, block_sem.at[slot, i]) for i, (a, b) in enumerate(pairs)]

    def tail_copies(t):
        pairs = sources(("tail", t), lambda d: tail.at[t, d])
        return [pltpu.make_async_copy(a, b, tail_sem.at[t, i]) for i, (a, b) in enumerate(pairs)]

    def row_copy(q):
        slot = q % 2
        return pltpu.make_async_copy(x.at[:, pl.ds(q * count, count), :], own_rows.at[slot], row_sem.at[slot])

    def load(q):
        @pl.when(polar == 1)
        def _():
            for c in main_copies(q):
                c.start()

        @pl.when(polar != 1)
        def _():
            row_copy(q).start()

    def prepare(q):
        place = q % 3

        @pl.when(polar == 1)
        def _():
            wait_all(main_copies(q))
            if q % 4 == 0:
                wait_all(tail_copies(q // 4))
            at = q % 4 * TAIL
            rows = jnp.concatenate([block[q % 2], tail[q // 4, :, :, at : at + TAIL]], axis=-1)
            field[place] = jnp.swapaxes(rows, 0, 1)[: cols + 2]

        @pl.when(polar != 1)
        def _():
            row_copy(q).wait()
            field[place, 1 : cols + 1] = own_rows[q % 2]
            field[place, :1] = sides[:1, q * count : (q + 1) * count]
            field[place, cols + 1 :] = sides[1:, q * count : (q + 1) * count]

    def store(q):
        return pltpu.make_async_copy(result.at[q % 2], out.at[:, pl.ds(q * count, count), :], out_sem.at[q % 2])

    @pl.when(polar == 1)
    def _():
        for t in range(tails):
            for c in tail_copies(t):
                c.start()

    load(0)
    load(1)
    prepare(0)
    spot = lax.broadcasted_iota(jnp.int32, (1, count, 1), 1)
    for q in range(tiles):
        if q + 2 < tiles:
            load(q + 2)
        if q + 1 < tiles:
            prepare(q + 1)
        if q >= 2:
            store(q - 2).wait()
        rows = slice(q * count, (q + 1) * count)
        k0, k1, k2, k3 = (coef[i, rows][None] for i in range(4))

        def step(i, carry):
            j = i * width
            f = field[q % 3, pl.ds(j, width + 2)].astype(F32)
            west, here, east = f[:-2], f[1:-1], f[2:]
            if q == 0:
                above = north[pl.ds(j, width)].astype(F32)
            else:
                above = field[(q - 1) % 3, pl.ds(j + 1, width)].astype(F32)
            if q == tiles - 1:
                below = south[pl.ds(j, width)].astype(F32)
            else:
                below = field[(q + 1) % 3, pl.ds(j + 1, width)].astype(F32)
            up = pltpu.roll(jnp.where(spot == count - 1, above, here), 1, 1)
            down = pltpu.roll(jnp.where(spot == 0, below, here), count - 1, 1)
            result[q % 2, pl.ds(j, width)] = k0 * here + k1 * (west + east) + (k2 * up + k3 * down)
            return carry

        lax.fori_loop(0, cols // width, step, 0)
        store(q).start()
    for q in range(max(tiles - 2, 0), tiles):
        store(q).wait()


def metric(global_rows, nlat):
    spacing = jnp.float32(math.pi / nlat)
    rows_f = global_rows.astype(jnp.float32)
    cell_cos = jnp.sin((rows_f + 0.5) * spacing)
    north_cos = jnp.where(global_rows == 0, jnp.float32(0.0), jnp.sin(rows_f * spacing))
    south_cos = jnp.where(global_rows == nlat - 1, jnp.float32(0.0), jnp.sin((rows_f + 1.0) * spacing))
    return (north_cos / cell_cos, south_cos / cell_cos)


def per_device(state, cutoff, viscosity):
    rows, cols, channels = state.shape
    lats = lax.axis_size("lat")
    count = lax.axis_size("lon")
    groups = count // 2
    nlat = rows * lats
    pad = -(-(cols + 2) // 8) * 8
    tiles = rows // count
    tails = tiles // 4
    lat, me = lax.axis_index("lat"), lax.axis_index("lon")
    edge = lats // 4
    is_polar = (lat < edge) | (lat >= lats - edge)
    flags = jnp.stack([me, is_polar.astype(jnp.int32)]).astype(jnp.int32)
    x = jnp.transpose(state, (1, 0, 2))

    helpers = [(i, i + edge) for i in range(edge)] + [(lats - 1 - i, lats - 1 - i - edge) for i in range(edge)]

    served = jnp.where(is_polar, lat, jnp.where(lat < lats // 2, lat - edge, lat + edge))
    served = jnp.where(served < lats // 2, served, served - lats // 2)
    cut_rows = lax.dynamic_slice_in_dim(cutoff, served * rows, rows)
    cut_mine = jnp.sum(
        jnp.where(jnp.arange(count)[None, :] == me, cut_rows.reshape(tiles, count), 0), axis=1
    )

    tables = []
    for parity in (0, 1):
        tables += [jnp.asarray(t) for t in table_pair(count, cols, pad, parity)]

    def block(n_blocks, lanes):
        return jax.ShapeDtypeStruct((n_blocks, pad, lanes), BF)

    def tie(value, *others):
        return lax.optimization_barrier((value, *others))[0] if others else value

    ran = []

    def call(kernel, arrays, specs, outs, name, scratch, after=(), out_specs=None):
        results = pl.pallas_call(
            kernel,
            in_specs=[IN_SMEM] + specs,
            out_specs=out_specs or [ANY] * len(outs),
            out_shape=outs,
            scratch_shapes=scratch,
            compiler_params=pltpu.CompilerParams(vmem_limit_bytes=60 * 2**20),
            cost_estimate=pl.CostEstimate(flops=1, bytes_accessed=1, transcendentals=0),
            name=name,
        )(tie(flags, *ran[-1:], *after), *arrays)
        ran.append(results[0])
        return results

    def sems(*shape):
        return pltpu.SemaphoreType.DMA(shape)

    def swapped(value):
        return lax.ppermute(value, "lon", [(i, i ^ 1) for i in range(count)])

    def pack(sets):
        units = [unit for group in sets for unit in group]
        size = sum(count if kind == "main" else 4 * count for kind, _ in units)
        shapes = [block(groups, MAIN * len(group)) for group in sets for _ in range(2)]
        outs = call(
            functools.partial(pack_kernel, cols, pad, count, sets), [x], [ANY], shapes, "pack",
            [
                pltpu.VMEM((cols, size, channels), BF), pltpu.VMEM((len(units), count, pad, MAIN), BF),
                sems(len(units)), sems(len(units) * count),
            ],
        )
        return [(outs[2 * u], outs[2 * u + 1]) for u in range(len(sets))]

    def hop(own, par, pairs):
        crossed = [(a * count + i, b * count + (i ^ 1)) for a, b in pairs for i in range(count)]
        return (lax.ppermute(own, "lat", pairs), lax.ppermute(par, ("lat", "lon"), crossed))

    def select(own, lifted=(), after=()):
        arrays = [*own, *lifted]
        lanes = own[0].shape[-1]
        return call(
            functools.partial(select_kernel, groups), arrays, [ANY] * len(arrays), [block(2, lanes)] * groups, "select",
            [pltpu.VMEM((groups, 2, pad, lanes), BF), sems(count), sems(groups)], after,
        )

    def cut_of(own_units, helped_units):
        def lanes_of(units):
            parts = []
            for kind, q in units:
                if kind == "main":
                    parts.append(jnp.broadcast_to(cut_mine[q], (MAIN,)))
                else:
                    parts.append(jnp.repeat(cut_mine[4 * q : 4 * q + 4], TAIL))
            return jnp.concatenate(parts)[None, :]

        own = lanes_of(own_units)
        return jnp.where(is_polar, own, lanes_of(helped_units)) if helped_units else own

    def run_filter(pieces, cut):
        lanes = cut.shape[-1]
        return call(
            functools.partial(filter_kernel, groups), [cut, *pieces, *tables], [IN_VMEM] + [ANY] * (groups + 4),
            [block(2, lanes)] * groups, "filter",
            [pltpu.VMEM((count, pad, lanes), BF)] * 2 + [pltpu.VMEM(t.shape, BF) for t in tables]
            + [sems(count), sems(4), sems(count)],
        )

    sent = []

    def exchange(pieces):
        got = [pieces[0]]
        for m in range(1, groups):
            value = tie(pieces[m], *(sent[1 - groups :][:1] if len(sent) >= groups - 1 else ()))
            sent.append(lax.ppermute(value, "lon", [(i, i ^ (2 * m)) for i in range(count)]))
            got.append(sent[-1])
        return got

    def gather(pieces):
        lanes = pieces[0].shape[-1]
        return call(
            functools.partial(gather_kernel, groups), pieces, [ANY] * groups, [block(groups, lanes)] * 2, "gather",
            [pltpu.VMEM((groups, 2, pad, lanes), BF), sems(groups), sems(count)],
        )

    mains = [("main", q) for q in range(tiles)]
    tail_units = [("tail", t) for t in range(tails)]
    order = [mains[tiles - 1], mains[0]] + mains[1 : tiles - 1]
    big = (tiles + tails) // 5
    helped = [order[:big], order[big : big + 1]]
    others = tail_units + order[big + 1 :]
    shared = [others[:big], others[big : big + 1]]
    lone = [others[i : i + big] for i in range(big + 1, len(others), big)]

    sides = jnp.concatenate(
        [
            lax.ppermute(x[cols - 1 :], "lon", [(i, (i + 1) % count) for i in range(count)]),
            lax.ppermute(x[:1], "lon", [((i + 1) % count, i) for i in range(count)]),
        ],
        axis=0,
    )

    back = [(b, a) for a, b in helpers]
    done, places = [], {}

    def finish(units, pair):
        for i, unit in enumerate(units):
            places[unit] = (len(done) // 2, i)
        done.extend(pair)

    def give(units, zs, helped_units=()):
        own, par = gather(zs)
        finish(units, (own, swapped(par)))
        if helped_units:
            finish(helped_units, hop(own, par, back))

    def apart(pair):
        return (pair[0], swapped(pair[1]))

    first_helped, first_lone = pack([helped[0], lone[0]])
    lifted = [hop(*first_helped, helpers)]
    got_lone = [exchange(select(apart(first_lone)))]
    later = pack(lone[1:] + shared + helped[1:])
    more_lone, own = later[: len(lone) - 1], later[len(lone) - 1 : len(lone) + 1]
    own = [apart(pair) for pair in own]
    more_lone = [apart(pair) for pair in more_lone]
    for pair in more_lone:
        got_lone.append(exchange(select(pair)))
    ys = select(own[0], lifted[0])
    lifted.append(hop(*(tie(v, ys[0]) for v in later[-1]), helpers))
    got = exchange(ys)
    z_lone = [run_filter(g, cut_of(units, [])) for g, units in zip(got_lone, lone)]
    zs = exchange(run_filter(got, cut_of(shared[0], helped[0])))
    ys = select(own[1], lifted[1])
    got = exchange(ys)
    give(shared[0], zs, helped[0])
    zs = exchange(run_filter(got, cut_of(shared[1], helped[1])))
    z_lone = [exchange([tie(v, ran[-1]) for v in z]) for z in z_lone]
    give(shared[1], zs, helped[1])
    for z, units in zip(z_lone, lone):
        give(units, z)

    edge_arrays, edge_specs = [], []
    for unit in (mains[0], mains[tiles - 1], tail_units[0], tail_units[tails - 1]):
        number, i = places[unit]
        edge_arrays += done[2 * number : 2 * number + 2]
        edge_specs += [pl.BlockSpec((groups, pad, MAIN), functools.partial(lambda k, i: (0, 0, k), i))] * 2

    def tile_spec(q):
        return pl.BlockSpec((cols, count, channels), lambda i: (0, q, 0))

    first, last = pl.pallas_call(
        functools.partial(edge_kernel, cols),
        grid=(1,),
        in_specs=[IN_SMEM] + edge_specs + [tile_spec(0), tile_spec(tiles - 1)],
        out_specs=[pl.BlockSpec((cols, channels), lambda i: (0, 0))] * 2,
        out_shape=[jax.ShapeDtypeStruct((cols, channels), BF)] * 2,
        compiler_params=pltpu.CompilerParams(vmem_limit_bytes=60 * 2**20),
        cost_estimate=pl.CostEstimate(flops=1, bytes_accessed=1, transcendentals=0),
        name="edges",
    )(flags, *edge_arrays, x, x)
    north = lax.ppermute(last, "lat", [(i, i + 1) for i in range(lats - 1)]).reshape(cols, 1, channels)
    south = lax.ppermute(first, "lat", [(i + 1, i) for i in range(lats - 1)]).reshape(cols, 1, channels)

    tile_rows = lat * rows + jnp.arange(rows, dtype=jnp.int32)
    north_ratio, south_ratio = metric(tile_rows, nlat)
    v = jnp.broadcast_to(viscosity[None, :], (rows, channels))
    a, b = north_ratio[:, None] * v, south_ratio[:, None] * v
    coef = jnp.stack([1.0 - 2.0 * v - a - b, v, a, b])

    updated = call(
        functools.partial(final_kernel, cols, count, tiles, places),
        [north, south, sides, coef, *done, x],
        [IN_VMEM] * 4 + [ANY] * (len(done) + 1),
        [jax.ShapeDtypeStruct((cols, rows, channels), F32)], "flux_step",
        [
            pltpu.VMEM((2, count, pad, MAIN), BF), pltpu.VMEM((tails, count, pad, MAIN), BF),
            pltpu.VMEM((2, cols, count, channels), BF), pltpu.VMEM((3, cols + 2, count, channels), BF),
            pltpu.VMEM((2, cols, count, channels), F32),
            sems(2, count), sems(tails, count), sems(2), sems(2),
        ],
    )[0]
    return jnp.transpose(updated, (1, 0, 2))


def solution(mesh):
    in_specs = (P("lat", "lon", None), P(), P())
    out_specs = P("lat", "lon", None)
    return jax.shard_map(per_device, mesh=mesh, in_specs=in_specs, out_specs=out_specs, check_vma=False)
```

```python
import functools
import math

import jax
import jax.numpy as jnp
import ml_dtypes
import numpy as np
from jax import lax
from jax.experimental import pallas as pl
from jax.experimental.pallas import tpu as pltpu
from jax.sharding import PartitionSpec as P

NLON = 1440
MAIN = 256
TAIL = 64
SMALL = 60
BF = jnp.bfloat16
F32 = jnp.float32
ANY = pl.BlockSpec(memory_space=pl.ANY)
IN_VMEM = pl.BlockSpec(memory_space=pltpu.VMEM)


def table_pair(count, cols, pad, parity):
    half = NLON // 2
    turns = np.arange(NLON, dtype=np.float32) * np.float32(2.0 * math.pi / NLON)
    cos, sin = np.cos(turns).astype(np.float32), np.sin(turns).astype(np.float32)
    even = np.arange(parity, half + 1, 2)
    odd = even[(even > 0) & (even < half)]
    modes = np.concatenate([even, odd])
    is_cos = np.arange(modes.size) < even.size

    def rows(extra):
        place, live = [], []
        for block in range(count // 2):
            base = block * cols - extra
            used = cols + 2 * extra
            place += [base + i for i in range(used)] + [0] * (pad - used)
            live += [1] * used + [0] * (pad - used)
        turn = (np.array(place)[:, None] % NLON) * modes[None, :] % NLON
        return np.where(is_cos[None, :], cos[turn], sin[turn]) * np.array(live, np.float32)[:, None]

    forward = np.ascontiguousarray(rows(0).T).astype(ml_dtypes.bfloat16)
    return forward, rows(1).astype(ml_dtypes.bfloat16)


def number():
    return lax.axis_index("lon")


def in_polar_tile():
    lat, lats = lax.axis_index("lat"), lax.axis_size("lat")
    return (lat < lats // 4) | (lat >= lats - lats // 4)


def copies(pairs, sems, base=0):
    made = [pltpu.make_async_copy(a, b, sems.at[base + i]) for i, (a, b) in enumerate(pairs)]
    for c in made:
        c.start()
    return made


def wait_all(made):
    for c in made:
        c.wait()


def pack_kernel(cols, pad, count, sets, *refs):
    me = number()
    n = len(sets)
    x, outs, (raw, work, in_sem, out_sem) = refs[0], refs[1 : 1 + 2 * n], refs[1 + 2 * n :]
    kinds = [(u, i, kind, q) for u, units in enumerate(sets) for i, (kind, q) in enumerate(units)]
    spots, at = [], 0
    for _, _, kind, q in kinds:
        size = count if kind == "main" else 4 * count
        spots.append((q * size, at, size))
        at += size
    loads = copies([(x.at[:, pl.ds(src, size), :], raw.at[:, pl.ds(dst, size), :]) for src, dst, size in spots], in_sem)
    stores = []
    for k, (u, i, kind, _) in enumerate(kinds):
        loads[k].wait()
        dst = spots[k][1]
        if kind == "main":
            flat = raw[:, dst : dst + count, :MAIN]
        else:
            flat = jnp.concatenate(
                [raw[:, dst + t * count : dst + (t + 1) * count, MAIN : MAIN + TAIL] for t in range(4)], axis=-1
            )
        turned = jnp.swapaxes(flat, 0, 1)
        for d in range(count):
            work[k, d, :cols] = turned[d]
            work[k, d, cols:] = jnp.zeros((pad - cols, MAIN), BF)
        lanes = pl.ds(i * MAIN, MAIN)
        pairs = []
        for m in range(count // 2):
            pairs.append((work.at[k, jnp.bitwise_xor(me, 2 * m)], outs[2 * u].at[m, :, lanes]))
            pairs.append((work.at[k, jnp.bitwise_xor(me, 2 * m + 1)], outs[2 * u + 1].at[m, :, lanes]))
        stores += copies(pairs, out_sem, k * count)
    wait_all(stores)


def select_kernel(groups, *refs):
    ins, ys, (held, in_sem, out_sem) = refs[: -groups - 3], refs[-groups - 3 : -3], refs[-3:]

    def move(own, par):
        spots = [(m, k) for m in range(groups) for k in range(2)]
        loads = copies([((own, par)[k].at[m], held.at[m, k]) for m, k in spots], in_sem)
        stores = []
        for m in range(groups):
            loads[2 * m].wait()
            loads[2 * m + 1].wait()
            stores += copies([(held.at[m], ys[m])], out_sem, m)
        wait_all(stores)

    if len(ins) == 2:
        move(*ins)
        return

    @pl.when(in_polar_tile())
    def _():
        move(*ins[:2])

    @pl.when(jnp.logical_not(in_polar_tile()))
    def _():
        move(*ins[2:])


def filter_kernel(groups, lane, cut, *refs):
    me = number()
    ins, tables, zs = refs[:groups], refs[groups : groups + 4], refs[groups + 4 : 2 * groups + 4]
    work, done, held, in_sem, table_sem, out_sem = refs[2 * groups + 4 :][0:2] + (refs[2 * groups + 6 : -3],) + refs[-3:]
    count, pad, lanes = work.shape
    half = count // 2
    pairs = []
    for m in range(groups):
        for k in range(2):
            pairs.append((ins[m].at[k], work.at[jnp.bitwise_xor(me, 2 * m + k)]))
    loads = copies(pairs, in_sem)
    table_loads = copies(list(zip(tables, held)), table_sem)
    wait_all(loads)
    low = work[:half].astype(F32)
    high = work[half:].astype(F32)
    cutoff = cut[:, lane : lane + lanes]

    def side(values, parity):
        values = values.reshape(half * pad, lanes).astype(BF)
        table_loads[2 * parity].wait()
        forward = held[2 * parity]
        spectrum = jnp.dot(forward[...], values, preferred_element_type=F32)
        index = lax.broadcasted_iota(jnp.int32, (forward.shape[0], 1), 0)
        cosines = NLON // 4 + 1 - parity
        mode = jnp.where(index < cosines, 2 * index + parity, 2 * (index - cosines) + 2 - parity)
        weight = jnp.where((mode == 0) | (mode == NLON // 2), F32(1.0 / NLON), F32(2.0 / NLON))
        damped = (spectrum * jnp.where(mode <= cutoff, weight, F32(0.0))).astype(BF)
        table_loads[2 * parity + 1].wait()
        return jnp.dot(held[2 * parity + 1][...], damped, preferred_element_type=F32)

    even = side(low + high, 0)
    odd = side(low - high, 1)
    done[:half] = (even + odd).reshape(half, pad, lanes).astype(BF)
    done[half:] = (even - odd).reshape(half, pad, lanes).astype(BF)
    pairs = []
    for m in range(groups):
        for k in range(2):
            pairs.append((done.at[jnp.bitwise_xor(me, 2 * m + k)], zs[m].at[k]))
    wait_all(copies(pairs, out_sem))


def gather_kernel(groups, *refs):
    ins, outs, (held, in_sem, out_sem) = refs[:groups], refs[groups : groups + 2], refs[groups + 2 :]
    loads = copies([(ins[m], held.at[m]) for m in range(groups)], in_sem)
    stores = []
    for m in range(groups):
        loads[m].wait()
        stores += copies([(held.at[m, k], outs[k].at[m]) for k in range(2)], out_sem, 2 * m)
    wait_all(stores)


def row_of(own, par, rel):
    spot = lax.shift_right_logical(rel, 1)
    return jnp.where(jnp.bitwise_and(rel, 1) == 0, own[spot], par[spot])


def edge_kernel(cols, fo, fp, lo, lp, fto, ftp, lto, ltp, x_first, x_last, out_first, out_last):
    me, polar = number(), in_polar_tile()
    count = x_first.shape[1]

    @pl.when(polar)
    def _():
        for spot, own, par, tail_own, tail_par, at, out in (
            (0, fo, fp, fto, ftp, 0, out_first),
            (count - 1, lo, lp, lto, ltp, MAIN - TAIL, out_last),
        ):
            rel = jnp.bitwise_xor(me, spot)
            out[...] = jnp.concatenate(
                [row_of(own, par, rel), row_of(tail_own, tail_par, rel)[:, at : at + TAIL]], axis=-1
            )[1 : cols + 1]

    @pl.when(jnp.logical_not(polar))
    def _():
        out_first[...] = x_first[:, 0, :]
        out_last[...] = x_last[:, count - 1, :]


def final_kernel(cols, count, tiles, span, places, north, south, sides, coef, *refs):
    tails = tiles // 4
    x, out = refs[0], refs[-10]
    parts = refs[1:]
    block, tail, own_rows, field, result, block_sem, tail_sem, row_sem, out_sem = refs[-9:]
    me, polar = number(), in_polar_tile()
    width = 15
    groups = count // 2
    begin, end = span
    first, last = max(begin - 1, 0), min(end + 1, tiles)

    def sources(unit, place):
        number, i = places[unit]
        lanes = pl.ds(i * MAIN, MAIN)
        pairs = []
        for m in range(groups):
            for k in range(2):
                pairs.append((parts[2 * number + k].at[m, :, lanes], place(jnp.bitwise_xor(me, 2 * m + k))))
        return pairs

    def main_copies(q):
        slot = q % 2
        pairs = sources(("main", q), lambda d: block.at[slot, d])
        return [pltpu.make_async_copy(a, b, block_sem.at[slot, i]) for i, (a, b) in enumerate(pairs)]

    def tail_copies(t):
        pairs = sources(("tail", t), lambda d: tail.at[t, d])
        return [pltpu.make_async_copy(a, b, tail_sem.at[t, i]) for i, (a, b) in enumerate(pairs)]

    def row_copy(q):
        slot = q % 2
        return pltpu.make_async_copy(x.at[:, pl.ds(q * count, count), :], own_rows.at[slot], row_sem.at[slot])

    def load(q):
        @pl.when(polar)
        def _():
            for c in main_copies(q):
                c.start()

        @pl.when(jnp.logical_not(polar))
        def _():
            row_copy(q).start()

    def prepare(q):
        place = q % 3

        @pl.when(polar)
        def _():
            wait_all(main_copies(q))
            if q == max(first, q // 4 * 4):
                wait_all(tail_copies(q // 4))
            at = q % 4 * TAIL
            rows = jnp.concatenate([block[q % 2], tail[q // 4, :, :, at : at + TAIL]], axis=-1)
            field[place] = jnp.swapaxes(rows, 0, 1)[: cols + 2]

        @pl.when(jnp.logical_not(polar))
        def _():
            row_copy(q).wait()
            field[place, 1 : cols + 1] = own_rows[q % 2]
            field[place, :1] = sides[:1, q * count : (q + 1) * count]
            field[place, cols + 1 :] = sides[1:, q * count : (q + 1) * count]

    def store(q):
        return pltpu.make_async_copy(result.at[q % 2], out.at[:, pl.ds(q * count, count), :], out_sem.at[q % 2])

    @pl.when(polar)
    def _():
        for t in range(first // 4, (last - 1) // 4 + 1):
            for c in tail_copies(t):
                c.start()

    load(first)
    load(first + 1)
    prepare(first)
    if first < begin:
        if first + 2 < last:
            load(first + 2)
        prepare(begin)
    spot = lax.broadcasted_iota(jnp.int32, (1, count, 1), 1)
    for q in range(begin, end):
        if q + 2 < last:
            load(q + 2)
        if q + 1 < last:
            prepare(q + 1)
        if q >= begin + 2:
            store(q - 2).wait()
        rows = slice(q * count, (q + 1) * count)
        k0, k1, k2, k3 = (coef[i, rows][None] for i in range(4))

        def step(i, carry):
            j = i * width
            f = field[q % 3, pl.ds(j, width + 2)].astype(F32)
            west, here, east = f[:-2], f[1:-1], f[2:]
            if q == 0:
                above = north[pl.ds(j, width)].astype(F32)
            else:
                above = field[(q - 1) % 3, pl.ds(j + 1, width)].astype(F32)
            if q == tiles - 1:
                below = south[pl.ds(j, width)].astype(F32)
            else:
                below = field[(q + 1) % 3, pl.ds(j + 1, width)].astype(F32)
            up = pltpu.roll(jnp.where(spot == count - 1, above, here), 1, 1)
            down = pltpu.roll(jnp.where(spot == 0, below, here), count - 1, 1)
            result[q % 2, pl.ds(j, width)] = k0 * here + k1 * (west + east) + (k2 * up + k3 * down)
            return carry

        lax.fori_loop(0, cols // width, step, 0)
        store(q).start()
    for q in range(max(end - 2, begin), end):
        store(q).wait()


def metric(global_rows, nlat):
    spacing = jnp.float32(math.pi / nlat)
    rows_f = global_rows.astype(jnp.float32)
    cell_cos = jnp.sin((rows_f + 0.5) * spacing)
    north_cos = jnp.where(global_rows == 0, jnp.float32(0.0), jnp.sin(rows_f * spacing))
    south_cos = jnp.where(global_rows == nlat - 1, jnp.float32(0.0), jnp.sin((rows_f + 1.0) * spacing))
    return (north_cos / cell_cos, south_cos / cell_cos)


def per_device(state, cutoff, viscosity):
    rows, cols, channels = state.shape
    lats = lax.axis_size("lat")
    count = lax.axis_size("lon")
    groups = count // 2
    nlat = rows * lats
    pad = -(-(cols + 2) // 8) * 8
    tiles = rows // count
    tails = tiles // 4
    lat, me = lax.axis_index("lat"), lax.axis_index("lon")
    edge = lats // 4
    is_polar = (lat < edge) | (lat >= lats - edge)
    x = jnp.transpose(state, (1, 0, 2))

    helpers = [(i, i + edge) for i in range(edge)] + [(lats - 1 - i, lats - 1 - i - edge) for i in range(edge)]

    back = [(b, a) for a, b in helpers]

    served = jnp.where(is_polar, lat, jnp.where(lat < lats // 2, lat - edge, lat + edge))
    served = jnp.where(served < lats // 2, served, served - lats // 2)
    cut_rows = lax.dynamic_slice_in_dim(cutoff, served * rows, rows)
    cut_mine = jnp.sum(
        jnp.where(jnp.arange(count)[None, :] == me, cut_rows.reshape(tiles, count), 0), axis=1
    )

    tables = []
    for parity in (0, 1):
        tables += [jnp.asarray(t) for t in table_pair(count, cols, pad, parity)]

    def block(n_blocks, lanes):
        return jax.ShapeDtypeStruct((n_blocks, pad, lanes), BF)

    def tie(value, *others):
        return lax.optimization_barrier((value, *others))[0] if others else value

    ran = []

    def call(kernel, arrays, specs, outs, name, scratch, after=(), mib=60, aliases=None):
        results = pl.pallas_call(
            kernel,
            in_specs=specs,
            out_specs=[ANY] * len(outs),
            out_shape=outs,
            scratch_shapes=scratch,
            compiler_params=pltpu.CompilerParams(vmem_limit_bytes=mib * 2**20),
            cost_estimate=pl.CostEstimate(flops=1, bytes_accessed=1, transcendentals=0),
            input_output_aliases=aliases or {},
            name=name,
        )(*arrays[:-1], tie(arrays[-1], *ran[-1:], *after))
        ran.append(results[0])
        return results

    def sems(*shape):
        return pltpu.SemaphoreType.DMA(shape)

    def swapped(value):
        return lax.ppermute(value, "lon", [(i, i ^ 1) for i in range(count)])

    def pack(sets, after=()):
        units = [unit for group in sets for unit in group]
        size = sum(count if kind == "main" else 4 * count for kind, _ in units)
        shapes = [block(groups, MAIN * len(group)) for group in sets for _ in range(2)]
        outs = call(
            functools.partial(pack_kernel, cols, pad, count, sets), [x], [ANY], shapes, "pack",
            [
                pltpu.VMEM((cols, size, channels), BF), pltpu.VMEM((len(units), count, pad, MAIN), BF),
                sems(len(units)), sems(len(units) * count),
            ],
            after,
        )
        return [(outs[2 * u], outs[2 * u + 1]) for u in range(len(sets))]

    def hop(own, par, pairs):
        crossed = [(a * count + i, b * count + (i ^ 1)) for a, b in pairs for i in range(count)]
        return (lax.ppermute(own, "lat", pairs), lax.ppermute(par, ("lat", "lon"), crossed))

    def select(own, lifted=(), after=()):
        arrays = [*own, *lifted]
        lanes = own[0].shape[-1]
        return call(
            functools.partial(select_kernel, groups), arrays, [ANY] * len(arrays), [block(2, lanes)] * groups, "select",
            [pltpu.VMEM((groups, 2, pad, lanes), BF), sems(count), sems(groups)], after, SMALL,
        )

    def run_filter(pieces, number, after=()):
        lanes = pieces[0].shape[-1]
        return call(
            functools.partial(filter_kernel, groups, cut_spot[number]), [cut_lanes, *pieces, *tables], [IN_VMEM] + [ANY] * (groups + 4),
            [block(2, lanes)] * groups, "filter",
            [pltpu.VMEM((count, pad, lanes), BF)] * 2 + [pltpu.VMEM(t.shape, BF) for t in tables]
            + [sems(count), sems(4), sems(count)], after, SMALL,
        )

    sent = []

    def exchange(pieces):
        got = [pieces[0]]
        for m in range(1, groups):
            value = tie(pieces[m], *(sent[1 - groups :][:1] if len(sent) >= groups - 1 else ()))
            sent.append(lax.ppermute(value, "lon", [(i, i ^ (2 * m)) for i in range(count)]))
            got.append(sent[-1])
        return got

    def gather(pieces, after=()):
        lanes = pieces[0].shape[-1]
        return call(
            functools.partial(gather_kernel, groups), pieces, [ANY] * groups, [block(groups, lanes)] * 2, "gather",
            [pltpu.VMEM((groups, 2, pad, lanes), BF), sems(groups), sems(count)], after, SMALL,
        )

    mains = [("main", q) for q in range(tiles)]
    tail_units = [("tail", t) for t in range(tails)]
    order = [mains[tiles - 1], mains[0]] + mains[1 : tiles - 1]
    big = (tiles + tails) // 5
    helped, others = order[:big], tail_units + order[big:]
    shared, lone, late = others[:big], others[big : 3 * big], others[3 * big :]

    rows_own, rows_help, cut_spot = [], [], []
    for units, served_units in [(shared, helped), (lone, lone), (late, late)]:
        cut_spot.append(len(rows_own))
        for listed, to in ((units, rows_own), (served_units, rows_help)):
            for kind, q in listed:
                to += [q] * MAIN if kind == "main" else [4 * q + i for i in range(4) for _ in range(TAIL)]
    row_lanes = jnp.where(is_polar, np.array(rows_own, np.int32), np.array(rows_help, np.int32))
    cut_lanes = jnp.sum(
        jnp.where(jnp.arange(tiles)[:, None] == row_lanes[None, :], cut_mine[:, None], 0), axis=0, keepdims=True
    )

    done, places = [], {}

    def finish(units, pair):
        for i, unit in enumerate(units):
            places[unit] = (len(done) // 2, i)
        done.extend(pair)

    def give(units, zs, after=()):
        own, par = gather(zs, after)
        finish(units, (own, swapped(par)))

    def apart(pair):
        return (pair[0], swapped(pair[1]))

    tile_rows = lat * rows + jnp.arange(rows, dtype=jnp.int32)
    north_ratio, south_ratio = metric(tile_rows, nlat)
    v = jnp.broadcast_to(viscosity[None, :], (rows, channels))
    a, b = north_ratio[:, None] * v, south_ratio[:, None] * v
    coef = jnp.stack([1.0 - 2.0 * v - a - b, v, a, b])

    def flux(span, below, so_far=()):
        return call(
            functools.partial(final_kernel, cols, count, tiles, span, dict(places)),
            [north, below, sides, coef, x, *done, *so_far],
            [IN_VMEM] * 4 + [ANY] * (len(done) + len(so_far) + 1),
            [jax.ShapeDtypeStruct((cols, rows, channels), F32)], "flux_step",
            [
                pltpu.VMEM((2, count, pad, MAIN), BF), pltpu.VMEM((tails, count, pad, MAIN), BF),
                pltpu.VMEM((2, cols, count, channels), BF), pltpu.VMEM((3, cols + 2, count, channels), BF),
                pltpu.VMEM((2, cols, count, channels), F32),
                sems(2, count), sems(tails, count), sems(2), sems(2),
            ],
            aliases={5 + len(done): 0} if so_far else {},
        )

    up, mine = pack([helped, lone])
    ys = select(apart(mine))
    got_lone = exchange(ys)
    lifted = hop(*(tie(v, ys[0]) for v in up), helpers)
    own, mine = pack([shared, late])
    own, mine = apart(own), apart(mine)
    got = exchange(select(own, lifted, got_lone[1:]))
    got_late = exchange(select(mine))
    z = exchange(run_filter(got, 0))
    z_lone = run_filter(got_lone, 1)
    own, par = gather(z)
    finish(shared, (own, swapped(par)))
    finish(helped, hop(own, par, back))
    z_lone = exchange(z_lone)
    z_late = run_filter(got_late, 2)
    give(lone, z_lone, done[2:4])
    sides = jnp.concatenate(
        [
            lax.ppermute(tie(x[cols - 1 :], ran[-1]), "lon", [(i, (i + 1) % count) for i in range(count)]),
            lax.ppermute(tie(x[:1], ran[-1]), "lon", [((i + 1) % count, i) for i in range(count)]),
        ],
        axis=0,
    )

    z_late = exchange(z_late)

    edge_arrays, edge_specs = [], []
    for unit in (mains[0], mains[tiles - 1], tail_units[0], tail_units[tails - 1]):
        number, i = places[unit]
        edge_arrays += done[2 * number : 2 * number + 2]
        edge_specs += [pl.BlockSpec((groups, pad, MAIN), functools.partial(lambda k, i: (0, 0, k), i))] * 2

    def tile_spec(q):
        return pl.BlockSpec((cols, count, channels), lambda i: (0, q, 0))

    first, last = pl.pallas_call(
        functools.partial(edge_kernel, cols),
        grid=(1,),
        in_specs=edge_specs + [tile_spec(0), tile_spec(tiles - 1)],
        out_specs=[pl.BlockSpec((cols, channels), lambda i: (0, 0))] * 2,
        out_shape=[jax.ShapeDtypeStruct((cols, channels), BF)] * 2,
        compiler_params=pltpu.CompilerParams(vmem_limit_bytes=60 * 2**20),
        cost_estimate=pl.CostEstimate(flops=1, bytes_accessed=1, transcendentals=0),
        name="edges",
    )(*edge_arrays, x, x)
    north = lax.ppermute(last, "lat", [(i, i + 1) for i in range(lats - 1)]).reshape(cols, 1, channels)
    south = lax.ppermute(first, "lat", [(i + 1, i) for i in range(lats - 1)]).reshape(cols, 1, channels)

    ready = 0
    while all(mains[q] in places for q in range(ready + 2)):
        ready += 1
    partly = flux((0, ready), north)
    give(late, z_late, [south])
    (updated,) = flux((ready, tiles), south, partly)

    return jnp.transpose(updated, (1, 0, 2))


def solution(mesh):
    in_specs = (P("lat", "lon", None), P(), P())
    out_specs = P("lat", "lon", None)
    return jax.shard_map(per_device, mesh=mesh, in_specs=in_specs, out_specs=out_specs, check_vma=False)
```

```python
import functools
import math

import jax
import jax.numpy as jnp
import ml_dtypes
import numpy as np
from jax import lax
from jax.experimental import pallas as pl
from jax.experimental.pallas import tpu as pltpu
from jax.sharding import PartitionSpec as P

NLON = 1440
MAIN = 256
TAIL = 64
SMALL = 60
BF = jnp.bfloat16
F32 = jnp.float32
ANY = pl.BlockSpec(memory_space=pl.ANY)
IN_VMEM = pl.BlockSpec(memory_space=pltpu.VMEM)


def table_pair(count, cols, pad, parity):
    half = NLON // 2
    turns = np.arange(NLON, dtype=np.float32) * np.float32(2.0 * math.pi / NLON)
    cos, sin = np.cos(turns).astype(np.float32), np.sin(turns).astype(np.float32)
    even = np.arange(parity, half + 1, 2)
    odd = even[(even > 0) & (even < half)]
    modes = np.concatenate([even, odd])
    is_cos = np.arange(modes.size) < even.size

    def rows(extra):
        place, live = [], []
        for block in range(count // 2):
            base = block * cols - extra
            used = cols + 2 * extra
            place += [base + i for i in range(used)] + [0] * (pad - used)
            live += [1] * used + [0] * (pad - used)
        turn = (np.array(place)[:, None] % NLON) * modes[None, :] % NLON
        return np.where(is_cos[None, :], cos[turn], sin[turn]) * np.array(live, np.float32)[:, None]

    forward = np.ascontiguousarray(rows(0).T).astype(ml_dtypes.bfloat16)
    return forward, rows(1).astype(ml_dtypes.bfloat16)


def number():
    return lax.axis_index("lon")


def in_polar_tile():
    lat, lats = lax.axis_index("lat"), lax.axis_size("lat")
    return (lat < lats // 4) | (lat >= lats - lats // 4)


def copies(pairs, sems, base=0):
    made = [pltpu.make_async_copy(a, b, sems.at[base + i]) for i, (a, b) in enumerate(pairs)]
    for c in made:
        c.start()
    return made


def wait_all(made):
    for c in made:
        c.wait()


def pack_kernel(cols, pad, count, sets, *refs):
    me = number()
    n = len(sets)
    x, outs, (raw, work, in_sem, out_sem) = refs[0], refs[1 : 1 + 2 * n], refs[1 + 2 * n :]
    kinds = [(u, i, kind, q) for u, units in enumerate(sets) for i, (kind, q) in enumerate(units)]
    spots, at = [], 0
    for _, _, kind, q in kinds:
        size = count if kind == "main" else 4 * count
        spots.append((q * size, at, size))
        at += size
    loads = copies([(x.at[:, pl.ds(src, size), :], raw.at[:, pl.ds(dst, size), :]) for src, dst, size in spots], in_sem)
    stores = []
    for k, (u, i, kind, _) in enumerate(kinds):
        loads[k].wait()
        dst = spots[k][1]
        if kind == "main":
            flat = raw[:, dst : dst + count, :MAIN]
        else:
            flat = jnp.concatenate(
                [raw[:, dst + t * count : dst + (t + 1) * count, MAIN : MAIN + TAIL] for t in range(4)], axis=-1
            )
        turned = jnp.swapaxes(flat, 0, 1)
        for d in range(count):
            work[k, d, :cols] = turned[d]
            work[k, d, cols:] = jnp.zeros((pad - cols, MAIN), BF)
        lanes = pl.ds(i * MAIN, MAIN)
        pairs = []
        for m in range(count // 2):
            pairs.append((work.at[k, jnp.bitwise_xor(me, 2 * m)], outs[2 * u].at[m, :, lanes]))
            pairs.append((work.at[k, jnp.bitwise_xor(me, 2 * m + 1)], outs[2 * u + 1].at[m, :, lanes]))
        stores += copies(pairs, out_sem, k * count)
    wait_all(stores)


def select_kernel(groups, *refs):
    ins, ys, (held, in_sem, out_sem) = refs[: -groups - 3], refs[-groups - 3 : -3], refs[-3:]

    def move(own, par):
        spots = [(m, k) for m in range(groups) for k in range(2)]
        loads = copies([((own, par)[k].at[m], held.at[m, k]) for m, k in spots], in_sem)
        stores = []
        for m in range(groups):
            loads[2 * m].wait()
            loads[2 * m + 1].wait()
            stores += copies([(held.at[m], ys[m])], out_sem, m)
        wait_all(stores)

    if len(ins) == 2:
        move(*ins)
        return

    @pl.when(in_polar_tile())
    def _():
        move(*ins[:2])

    @pl.when(jnp.logical_not(in_polar_tile()))
    def _():
        move(*ins[2:])


def filter_kernel(groups, lane, cut, *refs):
    me = number()
    ins, tables, zs = refs[:groups], refs[groups : groups + 4], refs[groups + 4 : 2 * groups + 4]
    work, done, held, in_sem, table_sem, out_sem = refs[2 * groups + 4 :][0:2] + (refs[2 * groups + 6 : -3],) + refs[-3:]
    count, pad, lanes = work.shape
    half = count // 2
    pairs = []
    for m in range(groups):
        for k in range(2):
            pairs.append((ins[m].at[k], work.at[jnp.bitwise_xor(me, 2 * m + k)]))
    loads = copies(pairs, in_sem)
    table_loads = copies(list(zip(tables, held)), table_sem)
    wait_all(loads)
    low = work[:half].astype(F32)
    high = work[half:].astype(F32)
    cutoff = cut[:, lane : lane + lanes]

    def side(values, parity):
        values = values.reshape(half * pad, lanes).astype(BF)
        table_loads[2 * parity].wait()
        forward = held[2 * parity]
        spectrum = jnp.dot(forward[...], values, preferred_element_type=F32)
        index = lax.broadcasted_iota(jnp.int32, (forward.shape[0], 1), 0)
        cosines = NLON // 4 + 1 - parity
        mode = jnp.where(index < cosines, 2 * index + parity, 2 * (index - cosines) + 2 - parity)
        weight = jnp.where((mode == 0) | (mode == NLON // 2), F32(1.0 / NLON), F32(2.0 / NLON))
        damped = (spectrum * jnp.where(mode <= cutoff, weight, F32(0.0))).astype(BF)
        table_loads[2 * parity + 1].wait()
        return jnp.dot(held[2 * parity + 1][...], damped, preferred_element_type=F32)

    even = side(low + high, 0)
    odd = side(low - high, 1)
    done[:half] = (even + odd).reshape(half, pad, lanes).astype(BF)
    done[half:] = (even - odd).reshape(half, pad, lanes).astype(BF)
    pairs = []
    for m in range(groups):
        for k in range(2):
            pairs.append((done.at[jnp.bitwise_xor(me, 2 * m + k)], zs[m].at[k]))
    wait_all(copies(pairs, out_sem))


def gather_kernel(groups, *refs):
    ins, outs, (held, in_sem, out_sem) = refs[:groups], refs[groups : groups + 2], refs[groups + 2 :]
    loads = copies([(ins[m], held.at[m]) for m in range(groups)], in_sem)
    stores = []
    for m in range(groups):
        loads[m].wait()
        stores += copies([(held.at[m, k], outs[k].at[m]) for k in range(2)], out_sem, 2 * m)
    wait_all(stores)


def row_of(own, par, rel):
    spot = lax.shift_right_logical(rel, 1)
    return jnp.where(jnp.bitwise_and(rel, 1) == 0, own[spot], par[spot])


def edge_kernel(cols, fo, fp, lo, lp, fto, ftp, lto, ltp, x_first, x_last, out_first, out_last):
    me, polar = number(), in_polar_tile()
    count = x_first.shape[1]

    @pl.when(polar)
    def _():
        for spot, own, par, tail_own, tail_par, at, out in (
            (0, fo, fp, fto, ftp, 0, out_first),
            (count - 1, lo, lp, lto, ltp, MAIN - TAIL, out_last),
        ):
            rel = jnp.bitwise_xor(me, spot)
            out[...] = jnp.concatenate(
                [row_of(own, par, rel), row_of(tail_own, tail_par, rel)[:, at : at + TAIL]], axis=-1
            )[1 : cols + 1]

    @pl.when(jnp.logical_not(polar))
    def _():
        out_first[...] = x_first[:, 0, :]
        out_last[...] = x_last[:, count - 1, :]


def final_kernel(cols, count, tiles, span, places, north, south, sides, coef, *refs):
    tails = tiles // 4
    x, out = refs[0], refs[-10]
    parts = refs[1:]
    block, tail, own_rows, field, result, block_sem, tail_sem, row_sem, out_sem = refs[-9:]
    me, polar = number(), in_polar_tile()
    width = 30
    groups = count // 2
    begin, end = span
    first, last = max(begin - 1, 0), min(end + 1, tiles)

    def sources(unit, place):
        number, i = places[unit]
        lanes = pl.ds(i * MAIN, MAIN)
        pairs = []
        for m in range(groups):
            for k in range(2):
                pairs.append((parts[2 * number + k].at[m, :, lanes], place(jnp.bitwise_xor(me, 2 * m + k))))
        return pairs

    def main_copies(q):
        slot = q % 2
        pairs = sources(("main", q), lambda d: block.at[slot, d])
        return [pltpu.make_async_copy(a, b, block_sem.at[slot, i]) for i, (a, b) in enumerate(pairs)]

    def tail_copies(t):
        pairs = sources(("tail", t), lambda d: tail.at[t, d])
        return [pltpu.make_async_copy(a, b, tail_sem.at[t, i]) for i, (a, b) in enumerate(pairs)]

    def row_copy(q):
        slot = q % 2
        return pltpu.make_async_copy(x.at[:, pl.ds(q * count, count), :], own_rows.at[slot], row_sem.at[slot])

    def load(q):
        @pl.when(polar)
        def _():
            for c in main_copies(q):
                c.start()

        @pl.when(jnp.logical_not(polar))
        def _():
            row_copy(q).start()

    def prepare(q):
        place = q % 3

        @pl.when(polar)
        def _():
            wait_all(main_copies(q))
            if q == max(first, q // 4 * 4):
                wait_all(tail_copies(q // 4))
            at = q % 4 * TAIL
            rows = jnp.concatenate([block[q % 2], tail[q // 4, :, :, at : at + TAIL]], axis=-1)
            field[place] = jnp.swapaxes(rows, 0, 1)[: cols + 2]

        @pl.when(jnp.logical_not(polar))
        def _():
            row_copy(q).wait()
            field[place, 1 : cols + 1] = own_rows[q % 2]
            field[place, :1] = sides[:1, q * count : (q + 1) * count]
            field[place, cols + 1 :] = sides[1:, q * count : (q + 1) * count]

    def store(q):
        return pltpu.make_async_copy(result.at[q % 2], out.at[:, pl.ds(q * count, count), :], out_sem.at[q % 2])

    @pl.when(polar)
    def _():
        for t in range(first // 4, (last - 1) // 4 + 1):
            for c in tail_copies(t):
                c.start()

    load(first)
    load(first + 1)
    prepare(first)
    if first < begin:
        if first + 2 < last:
            load(first + 2)
        prepare(begin)
    spot = lax.broadcasted_iota(jnp.int32, (1, count, 1), 1)
    for q in range(begin, end):
        if q + 2 < last:
            load(q + 2)
        if q + 1 < last:
            prepare(q + 1)
        if q >= begin + 2:
            store(q - 2).wait()
        rows = slice(q * count, (q + 1) * count)
        k0, k1, k2, k3 = (coef[i, rows][None] for i in range(4))

        def step(i, carry):
            j = i * width
            f = field[q % 3, pl.ds(j, width + 2)].astype(F32)
            west, here, east = f[:-2], f[1:-1], f[2:]
            if q == 0:
                above = north[pl.ds(j, width)].astype(F32)
            else:
                above = field[(q - 1) % 3, pl.ds(j + 1, width)].astype(F32)
            if q == tiles - 1:
                below = south[pl.ds(j, width)].astype(F32)
            else:
                below = field[(q + 1) % 3, pl.ds(j + 1, width)].astype(F32)
            up = pltpu.roll(jnp.where(spot == count - 1, above, here), 1, 1)
            down = pltpu.roll(jnp.where(spot == 0, below, here), count - 1, 1)
            result[q % 2, pl.ds(j, width)] = k0 * here + k1 * (west + east) + (k2 * up + k3 * down)
            return carry

        lax.fori_loop(0, cols // width, step, 0)
        store(q).start()
    for q in range(max(end - 2, begin), end):
        store(q).wait()


def metric(global_rows, nlat):
    spacing = jnp.float32(math.pi / nlat)
    rows_f = global_rows.astype(jnp.float32)
    cell_cos = jnp.sin((rows_f + 0.5) * spacing)
    north_cos = jnp.where(global_rows == 0, jnp.float32(0.0), jnp.sin(rows_f * spacing))
    south_cos = jnp.where(global_rows == nlat - 1, jnp.float32(0.0), jnp.sin((rows_f + 1.0) * spacing))
    return (north_cos / cell_cos, south_cos / cell_cos)


def per_device(state, cutoff, viscosity):
    rows, cols, channels = state.shape
    lats = lax.axis_size("lat")
    count = lax.axis_size("lon")
    groups = count // 2
    nlat = rows * lats
    pad = -(-(cols + 2) // 8) * 8
    tiles = rows // count
    tails = tiles // 4
    lat, me = lax.axis_index("lat"), lax.axis_index("lon")
    edge = lats // 4
    is_polar = (lat < edge) | (lat >= lats - edge)
    x = jnp.transpose(state, (1, 0, 2))

    helpers = [(i, i + edge) for i in range(edge)] + [(lats - 1 - i, lats - 1 - i - edge) for i in range(edge)]

    back = [(b, a) for a, b in helpers]

    served = jnp.where(is_polar, lat, jnp.where(lat < lats // 2, lat - edge, lat + edge))
    served = jnp.where(served < lats // 2, served, served - lats // 2)
    cut_rows = lax.dynamic_slice_in_dim(cutoff, served * rows, rows)
    cut_mine = jnp.sum(
        jnp.where(jnp.arange(count)[None, :] == me, cut_rows.reshape(tiles, count), 0), axis=1
    )

    tables = []
    for parity in (0, 1):
        tables += [jnp.asarray(t) for t in table_pair(count, cols, pad, parity)]

    def block(n_blocks, lanes):
        return jax.ShapeDtypeStruct((n_blocks, pad, lanes), BF)

    def tie(value, *others):
        return lax.optimization_barrier((value, *others))[0] if others else value

    ran = []

    def call(kernel, arrays, specs, outs, name, scratch, after=(), mib=60, aliases=None):
        results = pl.pallas_call(
            kernel,
            in_specs=specs,
            out_specs=[ANY] * len(outs),
            out_shape=outs,
            scratch_shapes=scratch,
            compiler_params=pltpu.CompilerParams(vmem_limit_bytes=mib * 2**20),
            cost_estimate=pl.CostEstimate(flops=1, bytes_accessed=1, transcendentals=0),
            input_output_aliases=aliases or {},
            name=name,
        )(*arrays[:-1], tie(arrays[-1], *ran[-1:], *after))
        ran.append(results[0])
        return results

    def sems(*shape):
        return pltpu.SemaphoreType.DMA(shape)

    def swapped(value):
        return lax.ppermute(value, "lon", [(i, i ^ 1) for i in range(count)])

    def pack(sets, after=()):
        units = [unit for group in sets for unit in group]
        size = sum(count if kind == "main" else 4 * count for kind, _ in units)
        shapes = [block(groups, MAIN * len(group)) for group in sets for _ in range(2)]
        outs = call(
            functools.partial(pack_kernel, cols, pad, count, sets), [x], [ANY], shapes, "pack",
            [
                pltpu.VMEM((cols, size, channels), BF), pltpu.VMEM((len(units), count, pad, MAIN), BF),
                sems(len(units)), sems(len(units) * count),
            ],
            after,
        )
        return [(outs[2 * u], outs[2 * u + 1]) for u in range(len(sets))]

    def hop(own, par, pairs):
        crossed = [(a * count + i, b * count + (i ^ 1)) for a, b in pairs for i in range(count)]
        return (lax.ppermute(own, "lat", pairs), lax.ppermute(par, ("lat", "lon"), crossed))

    def select(own, lifted=(), after=()):
        arrays = [*own, *lifted]
        lanes = own[0].shape[-1]
        return call(
            functools.partial(select_kernel, groups), arrays, [ANY] * len(arrays), [block(2, lanes)] * groups, "select",
            [pltpu.VMEM((groups, 2, pad, lanes), BF), sems(count), sems(groups)], after, SMALL,
        )

    def run_filter(pieces, number, after=()):
        lanes = pieces[0].shape[-1]
        return call(
            functools.partial(filter_kernel, groups, cut_spot[number]), [cut_lanes, *pieces, *tables], [IN_VMEM] + [ANY] * (groups + 4),
            [block(2, lanes)] * groups, "filter",
            [pltpu.VMEM((count, pad, lanes), BF)] * 2 + [pltpu.VMEM(t.shape, BF) for t in tables]
            + [sems(count), sems(4), sems(count)], after, SMALL,
        )

    sent = []

    def exchange(pieces):
        got = [pieces[0]]
        for m in range(1, groups):
            value = tie(pieces[m], *(sent[1 - groups :][:1] if len(sent) >= groups - 1 else ()))
            sent.append(lax.ppermute(value, "lon", [(i, i ^ (2 * m)) for i in range(count)]))
            got.append(sent[-1])
        return got

    def gather(pieces, after=()):
        lanes = pieces[0].shape[-1]
        return call(
            functools.partial(gather_kernel, groups), pieces, [ANY] * groups, [block(groups, lanes)] * 2, "gather",
            [pltpu.VMEM((groups, 2, pad, lanes), BF), sems(groups), sems(count)], after, SMALL,
        )

    mains = [("main", q) for q in range(tiles)]
    tail_units = [("tail", t) for t in range(tails)]
    order = [mains[tiles - 1], mains[0]] + mains[1 : tiles - 1]
    big = (tiles + tails) // 5
    helped, others = order[:big], tail_units + order[big:]
    shared, lone, late = others[:big], others[big : 3 * big], others[3 * big :]

    rows_own, rows_help, cut_spot = [], [], []
    for units, served_units in [(shared, helped), (lone, lone), (late, late)]:
        cut_spot.append(len(rows_own))
        for listed, to in ((units, rows_own), (served_units, rows_help)):
            for kind, q in listed:
                to += [q] * MAIN if kind == "main" else [4 * q + i for i in range(4) for _ in range(TAIL)]
    row_lanes = jnp.where(is_polar, np.array(rows_own, np.int32), np.array(rows_help, np.int32))
    cut_lanes = jnp.sum(
        jnp.where(jnp.arange(tiles)[:, None] == row_lanes[None, :], cut_mine[:, None], 0), axis=0, keepdims=True
    )

    done, places = [], {}

    def finish(units, pair):
        for i, unit in enumerate(units):
            places[unit] = (len(done) // 2, i)
        done.extend(pair)

    def give(units, zs, after=()):
        own, par = gather(zs, after)
        finish(units, (own, swapped(par)))

    def apart(pair):
        return (pair[0], swapped(pair[1]))

    tile_rows = lat * rows + jnp.arange(rows, dtype=jnp.int32)
    north_ratio, south_ratio = metric(tile_rows, nlat)
    v = jnp.broadcast_to(viscosity[None, :], (rows, channels))
    a, b = north_ratio[:, None] * v, south_ratio[:, None] * v
    coef = jnp.stack([1.0 - 2.0 * v - a - b, v, a, b])

    def flux(span, below, so_far=()):
        return call(
            functools.partial(final_kernel, cols, count, tiles, span, dict(places)),
            [north, below, sides, coef, x, *done, *so_far],
            [IN_VMEM] * 4 + [ANY] * (len(done) + len(so_far) + 1),
            [jax.ShapeDtypeStruct((cols, rows, channels), F32)], "flux_step",
            [
                pltpu.VMEM((2, count, pad, MAIN), BF), pltpu.VMEM((tails, count, pad, MAIN), BF),
                pltpu.VMEM((2, cols, count, channels), BF), pltpu.VMEM((3, cols + 2, count, channels), BF),
                pltpu.VMEM((2, cols, count, channels), F32),
                sems(2, count), sems(tails, count), sems(2), sems(2),
            ],
            aliases={5 + len(done): 0} if so_far else {},
        )

    up, mine = pack([helped, lone])
    lifted = hop(*up, helpers)
    ys = select(apart(mine))
    got_lone = exchange(ys)
    own, mine = pack([shared, late])
    own, mine = apart(own), apart(mine)
    got = exchange(select(own, lifted, got_lone[1:]))
    got_late = exchange(select(mine))
    z = exchange(run_filter(got, 0))
    z_lone = run_filter(got_lone, 1)
    own, par = gather(z)
    finish(shared, (own, swapped(par)))
    finish(helped, hop(own, par, back))
    z_lone = exchange(z_lone)
    z_late = run_filter(got_late, 2)
    give(lone, z_lone, done[2:4])
    sides = jnp.concatenate(
        [
            lax.ppermute(tie(x[cols - 1 :], ran[-1]), "lon", [(i, (i + 1) % count) for i in range(count)]),
            lax.ppermute(tie(x[:1], ran[-1]), "lon", [((i + 1) % count, i) for i in range(count)]),
        ],
        axis=0,
    )

    z_late = exchange(z_late)

    edge_arrays, edge_specs = [], []
    for unit in (mains[0], mains[tiles - 1], tail_units[0], tail_units[tails - 1]):
        number, i = places[unit]
        edge_arrays += done[2 * number : 2 * number + 2]
        edge_specs += [pl.BlockSpec((groups, pad, MAIN), functools.partial(lambda k, i: (0, 0, k), i))] * 2

    def tile_spec(q):
        return pl.BlockSpec((cols, count, channels), lambda i: (0, q, 0))

    first, last = pl.pallas_call(
        functools.partial(edge_kernel, cols),
        grid=(1,),
        in_specs=edge_specs + [tile_spec(0), tile_spec(tiles - 1)],
        out_specs=[pl.BlockSpec((cols, channels), lambda i: (0, 0))] * 2,
        out_shape=[jax.ShapeDtypeStruct((cols, channels), BF)] * 2,
        compiler_params=pltpu.CompilerParams(vmem_limit_bytes=60 * 2**20),
        cost_estimate=pl.CostEstimate(flops=1, bytes_accessed=1, transcendentals=0),
        name="edges",
    )(*edge_arrays, x, x)
    north = lax.ppermute(last, "lat", [(i, i + 1) for i in range(lats - 1)]).reshape(cols, 1, channels)
    south = lax.ppermute(first, "lat", [(i + 1, i) for i in range(lats - 1)]).reshape(cols, 1, channels)

    ready = 0
    while all(mains[q] in places for q in range(ready + 2)):
        ready += 1
    partly = flux((0, ready), north)
    give(late, z_late, [south])
    (updated,) = flux((ready, tiles), south, partly)

    return jnp.transpose(updated, (1, 0, 2))


def solution(mesh):
    in_specs = (P("lat", "lon", None), P(), P())
    out_specs = P("lat", "lon", None)
    return jax.shard_map(per_device, mesh=mesh, in_specs=in_specs, out_specs=out_specs, check_vma=False)
```
